128 devices in a mesh: row: 4 (over x), col: 8 (over y, core), layer: 4 (over z).
Axes of the slice: x: 4, y: 4, z: 4, core: 2. Of those that a mesh axis runs over, the one named last changes fastest.
Arguments:
- blocks: bfloat16 [512, 16, 128, 128], P(('row', 'col')), may hold values from -0.125 to 0.125
- flags: int32 [512, 16], P(('row', 'col')), may hold values 0 or 1
Outputs:
- next_blocks: bfloat16 [512, 16, 128, 128], P(('row', 'col', 'layer'))
The draws below stay inside these ranges and needn't reach their ends.
All inputs are finite; a program needn't handle non-finite values. No bound on the sum of `flags` on one device may be relied on, other than what follows from the above.
Results may differ from the reference program's by a relative error of at most 0.0075.
Values may be sent and summed in bfloat16 or wider, within the bound.
A program may use at most 192 MiB of HBM per device.

```python
import jax
import jax.numpy as jnp
from jax import lax

BS = 128
W = 16
NB = 512


def with_ends(array, rng, smallest, high):
    longest = array.shape.index(max(array.shape))
    spots = []
    for shift in (0, 1):
        where = [jax.random.randint(jax.random.fold_in(rng, axis), (), 0, length) for axis, length in enumerate(array.shape)]
        where[longest] = (where[longest] + shift) % array.shape[longest]
        spots.append(tuple(where))
    return array.at[spots[0]].set(smallest).at[spots[1]].set(high)


def level_of(own_key, extent, pieces, smallest, largest):
    loudness, own = 1.0, jax.random.fold_in(own_key, 6)
    for axis_at, blocks in pieces:
        draws = jnp.exp(jax.random.uniform(jax.random.fold_in(own, axis_at), (blocks,), jnp.float32, smallest / len(pieces), largest / len(pieces)))
        loudness = loudness * jnp.repeat(draws, extent[axis_at] // blocks).reshape([-1 if axis == axis_at else 1 for axis in range(len(extent))])
    return loudness


def normal_values(stream_key, dims, deviation, most, pieces=(), kind=jnp.bfloat16):
    entries = jax.random.normal(stream_key, dims, jnp.float32) * deviation
    if len(pieces) > 0:
        entries = level_of(stream_key, dims, pieces, -0.22, 0.18) * entries
    return jnp.clip(entries, min=-most, max=most).astype(kind)


def setup_inputs(seed: int = 0) -> dict:
    keys = jax.random.split(jax.random.key(seed), 3)
    return {
        "blocks": normal_values(keys[0], (NB, W, BS, BS), (W * BS) ** -0.5, 0.125, ((0, 32),)),
        "flags": with_ends((jax.random.randint(keys[1], (NB, W), 0, 4) < 3).astype(jnp.int32), jax.random.fold_in(keys[1], 1), 0, 1),
    }


def keep_of(flags):
    slots = jnp.arange(W, dtype=jnp.int32)
    centre = (slots == W // 2).astype(jnp.int32)
    return jnp.maximum(flags, centre[None, :]).astype(jnp.float32)[:, :, None, None]


def banded_product(left, right):
    half = W // 2
    wrapped = jnp.concatenate([right[NB - half:], right, right[:half]], axis=0)
    padded = jnp.pad(wrapped, ((0, 0), (W, W), (0, 0), (0, 0)))

    def step(slot, total):
        offset = slot - half
        piece = lax.dynamic_slice_in_dim(left, slot, 1, 1)[:, 0].astype(jnp.float32)
        moved = lax.dynamic_slice(padded, (offset + half, W - offset, 0, 0), (NB, W, BS, BS)).astype(jnp.float32)
        return total + jnp.einsum('nxy,nsyz->nsxz', piece, moved)

    start = jnp.zeros((NB, W, BS, BS), jnp.float32)
    return lax.fori_loop(0, W, step, start)


def reference(blocks, flags):
    keep = keep_of(flags)
    filtered = (blocks.astype(jnp.float32) * keep).astype(jnp.bfloat16)
    square = banded_product(filtered, filtered) * keep
    slots = jnp.arange(W, dtype=jnp.int32)
    ident = jnp.where((slots == W // 2)[:, None, None], jnp.eye(BS, dtype=jnp.float32)[None], jnp.float32(0.0))
    third = (3.0 * ident[None] - square).astype(jnp.bfloat16)
    result = 0.5 * banded_product(filtered, third) * keep
    return result.astype(jnp.bfloat16)
```

```python
import functools

import jax
import jax.numpy as jnp
from jax import lax
from jax.experimental import pallas as pl
from jax.experimental.pallas import tpu as pltpu
from jax.sharding import PartitionSpec as P

MESH = pl.DeviceIdType.MESH
REACH = 4
DIAGS = range(-REACH, REACH + 1)
BS = 128
SB = 256
W = 16


def place(layer, kind, d):
    m = (d - layer + 3) >> 2
    t = (m + kind) & 1
    return layer - d + 4 * m + 4 * t, 1 + m + t


def spans(d):
    out = []
    for r in range(2):
        low, high = 2 * d - r + 8, 2 * d - r + 10
        first, last = max(low, 0), min(high, W)
        if last > first:
            out.append((r, first - low, first, last - first))
    return out


def kernel(x, flags, out, xc, xs, xl, xr, tr, os, load_c, load_x, send_x, recv_x, send_t, recv_t, send_o, recv_o, own_o):
    row, col, layer = lax.axis_index("row"), lax.axis_index("col"), lax.axis_index("layer")
    cols, layers = lax.axis_size("col"), lax.axis_size("layer")
    groups = lax.axis_size("row") * cols
    group = row * cols + col

    def at_group(step):
        there = lax.rem(group + step + groups, groups)
        return there // cols, lax.rem(there, cols), layer

    above, below = at_group(1), at_group(-1)

    def keep(i, s):
        return jnp.float32(1.0) if s == W // 2 else flags[i, s].astype(jnp.float32)

    def class_loads(kind):
        for d in DIAGS:
            i, _ = place(layer, kind, d)
            for r, q, s, n in spans(d):
                yield pltpu.make_async_copy(
                    x.at[2 * i + r, pl.ds(s, n)], xc.at[kind, d + REACH, r, pl.ds(q, n)], load_c.at[kind]
                )

    for kind in range(2):
        for copy in class_loads(kind):
            copy.start()

    def big_load(i):
        return pltpu.make_async_copy(x.at[pl.ds(2 * i, 2)], xs.at[pl.ds(2 * i, 2)], load_x.at[i])

    for i in range(8):
        big_load(i).start()

    for ref in (xr, tr):
        ref[1, pl.ds(layer * SB, SB), :] = jnp.zeros((SB, SB), jnp.bfloat16)

    barrier = pltpu.get_barrier_semaphore()
    for there in (above, below):
        pl.semaphore_signal(barrier, inc=1, device_id=there, device_id_type=MESH)
    for k in range(1, layers):
        there = (row, col, lax.rem(layer + k, layers))
        pl.semaphore_signal(barrier, inc=1, device_id=there, device_id_type=MESH)
    pl.semaphore_wait(barrier, 2 + layers - 1)

    def halo(ref, send, recv, kind, d):
        i, c = place(layer, kind, d)

        def copy(to, c_there, i_there, n):
            high, wide = (SB // 2, BS) if d == REACH else (SB, SB)
            shift = SB - high
            return pltpu.make_async_remote_copy(
                src_ref=ref.at[c, pl.ds((i + 4) * SB + shift, high), pl.ds(0, wide)],
                dst_ref=ref.at[c_there, pl.ds(i_there * SB + shift, high), pl.ds(0, wide)],
                send_sem=send.at[n, kind, d + REACH],
                recv_sem=recv.at[n, kind, d + REACH],
                device_id=to,
                device_id_type=MESH,
            )

        if d > -REACH:
            yield (c >= 2) & (i >= 4), lambda: copy(above, c - 2, i - 4, 0)
        if d < REACH:
            yield (c <= 1) & (i <= 3), lambda: copy(below, c + 2, i + 12, 1)

    def halo_do(ref, send, recv, kind, d, act):
        for cond, make in halo(ref, send, recv, kind, d):
            pl.when(cond)(functools.partial(lambda make: getattr(make(), act)(), make))

    def masked(block, k):
        return block * jnp.full(block.shape, k, jnp.float32).astype(jnp.bfloat16)

    for kind in range(2):
        pltpu.make_async_copy(x.at[pl.ds(0, 2)], xs.at[pl.ds(0, 2)], load_c.at[kind]).wait()
        for d in DIAGS:
            i, c = place(layer, kind, d)
            if abs(d) == REACH:
                xr[c, pl.ds((i + 4) * SB, SB), :] = jnp.zeros((SB, SB), jnp.bfloat16)
            for r, q0, s0, n in spans(d):
                for q, s in zip(range(q0, q0 + n), range(s0, s0 + n)):
                    xr[c, pl.ds((i + 4) * SB + r * BS, BS), pl.ds(q * BS, BS)] = masked(
                        xc[kind, d + REACH, r, q], keep(2 * i + r, s)
                    )
            halo_do(xr, send_x, recv_x, kind, d, "start")

    def fill(i, _):
        big_load(i).wait()
        none = jnp.zeros((BS, BS), jnp.bfloat16)
        for r in range(2):
            for s in range(W):
                xl[i, pl.ds(r * BS, BS), pl.ds((r + s) * BS, BS)] = masked(xs[2 * i + r, s], keep(2 * i + r, s))
        xl[i, pl.ds(0, BS), pl.ds(16 * BS, BS)] = none
        xl[i, pl.ds(0, BS), pl.ds(17 * BS, BS)] = none
        xl[i, pl.ds(BS, BS), pl.ds(0, BS)] = none
        xl[i, pl.ds(BS, BS), pl.ds(17 * BS, BS)] = none
        return 0

    lax.fori_loop(0, 8, fill, 0)

    def product(ref, i, c, d):
        n, first = 9 - abs(d), max(d, 0)
        return jnp.dot(
            xl[i, :, pl.ds(first * SB, n * SB)],
            ref[c, pl.ds((i + first) * SB, n * SB), :],
            preferred_element_type=jnp.float32,
        )

    rows_at = lax.broadcasted_iota(jnp.int32, (BS, BS), 0)
    cols_at = lax.broadcasted_iota(jnp.int32, (BS, BS), 1)

    def first_product(kind, _):
        for d in DIAGS:
            halo_do(xr, send_x, recv_x, kind, d, "wait_recv")
        three = jnp.where(rows_at == cols_at, jnp.float32(3.0), jnp.float32(0.0))
        for d in DIAGS:
            i, c = place(layer, kind, d)
            total = product(xr, i, c, d)
            if abs(d) == REACH:
                tr[c, pl.ds((i + 4) * SB, SB), :] = jnp.zeros((SB, SB), jnp.bfloat16)
            for r, q0, s0, n in spans(d):
                for q, s in zip(range(q0, q0 + n), range(s0, s0 + n)):
                    part = total[r * BS : (r + 1) * BS, q * BS : (q + 1) * BS]
                    part = three - part if s == W // 2 else part * -keep(2 * i + r, s)
                    tr[c, pl.ds((i + 4) * SB + r * BS, BS), pl.ds(q * BS, BS)] = part.astype(jnp.bfloat16)
            halo_do(tr, send_t, recv_t, kind, d, "start")
        return 0

    lax.fori_loop(0, 2, first_product, 0)

    def second_product(kind, _):
        for d in DIAGS:
            halo_do(tr, send_t, recv_t, kind, d, "wait_recv")
        for d in DIAGS:
            i, c = place(layer, kind, d)
            total = product(tr, i, c, d)
            owner = i >> 1
            for r, q0, s0, n in spans(d):
                for q, s in zip(range(q0, q0 + n), range(s0, s0 + n)):
                    part = total[r * BS : (r + 1) * BS, q * BS : (q + 1) * BS]
                    os[kind, d + REACH, r, q] = (part * (0.5 * keep(2 * i + r, s))).astype(jnp.bfloat16)

            @pl.when(owner == layer)
            def _():
                for r, q, s, n in spans(d):
                    pltpu.make_async_copy(
                        os.at[kind, d + REACH, r, pl.ds(q, n)], out.at[2 * (i & 1) + r, pl.ds(s, n)], own_o
                    ).start()

            @pl.when(owner != layer)
            def _():
                for r, q, s, n in spans(d):
                    pltpu.make_async_remote_copy(
                        src_ref=os.at[kind, d + REACH, r, pl.ds(q, n)],
                        dst_ref=out.at[2 * (i & 1) + r, pl.ds(s, n)],
                        send_sem=send_o,
                        recv_sem=recv_o,
                        device_id=(row, col, owner),
                        device_id_type=MESH,
                    ).start()
        return 0

    lax.fori_loop(0, 2, second_product, 0)

    pltpu.make_async_copy(xs.at[pl.ds(0, 1)], out.at[pl.ds(0, 1)], own_o).wait()
    pltpu.make_async_copy(xs.at[pl.ds(0, 3)], out.at[pl.ds(0, 3)], send_o).wait()
    pltpu.make_async_copy(xs.at[pl.ds(0, 3)], out.at[pl.ds(0, 3)], recv_o).wait()

    def sent(kind, _):
        for d in DIAGS:
            halo_do(xr, send_x, recv_x, kind, d, "wait_send")
            halo_do(tr, send_t, recv_t, kind, d, "wait_send")
        return 0

    lax.fori_loop(0, 2, sent, 0)


def per_device(blocks, flags):
    halos = pltpu.SemaphoreType.DMA((2, 2, 9))
    return pl.pallas_call(
        kernel,
        out_shape=jax.ShapeDtypeStruct((4, W, BS, BS), jnp.bfloat16),
        in_specs=[pl.BlockSpec(memory_space=pl.ANY), pl.BlockSpec(memory_space=pltpu.SMEM)],
        out_specs=pl.BlockSpec(memory_space=pl.ANY),
        scratch_shapes=[
            pltpu.VMEM((2, 9, 2, 2, BS, BS), jnp.bfloat16),
            pltpu.VMEM((16, W, BS, BS), jnp.bfloat16),
            pltpu.VMEM((8, SB, 9 * SB), jnp.bfloat16),
            pltpu.VMEM((4, 16 * SB, SB), jnp.bfloat16),
            pltpu.VMEM((4, 16 * SB, SB), jnp.bfloat16),
            pltpu.VMEM((2, 9, 2, 2, BS, BS), jnp.bfloat16),
            pltpu.SemaphoreType.DMA((2,)),
            pltpu.SemaphoreType.DMA((8,)),
            halos,
            halos,
            halos,
            halos,
            pltpu.SemaphoreType.DMA,
            pltpu.SemaphoreType.DMA,
            pltpu.SemaphoreType.DMA,
        ],
        compiler_params=pltpu.CompilerParams(
            collective_id=0, has_side_effects=True, vmem_limit_bytes=56 * 2**20
        ),
        cost_estimate=pl.CostEstimate(
            flops=2 * 2 * 122 * SB**3, bytes_accessed=10 * 2**20, transcendentals=0
        ),
    )(blocks, flags)


def solution(mesh):
    return jax.shard_map(
        per_device,
        mesh=mesh,
        in_specs=(P(("row", "col"), None, None, None), P(("row", "col"), None)),
        out_specs=P(("row", "col", "layer"), None, None, None),
        check_vma=False,
    )
```

```python
import functools

import jax
import jax.numpy as jnp
from jax import lax
from jax.experimental import pallas as pl
from jax.experimental.pallas import tpu as pltpu
from jax.sharding import PartitionSpec as P

MESH = pl.DeviceIdType.MESH
REACH = 4
DIAGS = range(-REACH, REACH + 1)
BS = 128
SB = 256
W = 16
ROWS = 16


ORDERS = (
    ((3, 0), (2, 0), (1, 0), (3, 1), (2, 1), (0, 0), (1, 1), (0, 1)),
    ((0, 0), (1, 0), (3, 0), (0, 1), (1, 1), (2, 0), (3, 1), (2, 1)),
)


def place(layer, kind, d):
    m = (d - layer + 3) >> 2
    t = (m + kind) & 1
    return layer - d + 4 * m + 4 * t, 1 + m + t


def spans(d):
    out = []
    for r in range(2):
        low, high = 2 * d - r + 8, 2 * d - r + 10
        first, last = max(low, 0), min(high, W)
        if last > first:
            out.append((r, first - low, first, last - first))
    return out


def cells(d):
    return [(r, q0 + k, s0 + k) for r, q0, s0, n in spans(d) for k in range(n)]


def chain(layer, c):
    middle = layer - 4 + 4 * c
    return [(1 - c % 2, middle - i) for i in range(max(middle - 4, 0), min(middle + 4, 7) + 1)]


def way_of(layer, kind, d):
    i, c = place(layer, kind, d)
    if c >= 2 and i >= 4:
        return 0, c - 2, i - 8
    if c <= 1 and i <= 3:
        return 1, c + 2, i + 8
    return None


def kernel(
    x, flags, flags_any, out, hx, xs, xl, right, res, flags_by, load_x,
    send_f, recv_f, send_x, recv_x, send_t, recv_t, send_o, recv_o, own_o,
):
    row, col, layer = lax.axis_index("row"), lax.axis_index("col"), lax.axis_index("layer")
    cols, layers = lax.axis_size("col"), lax.axis_size("layer")
    groups = lax.axis_size("row") * cols
    group = row * cols + col

    def at_group(step):
        there = lax.rem(group + step + groups, groups)
        return there // cols, lax.rem(there, cols), layer

    sides = at_group(1), at_group(-1)

    def keep(i, s):
        return jnp.float32(1.0) if s == W // 2 else flags[i, s].astype(jnp.float32)

    def big_load(i):
        return pltpu.make_async_copy(x.at[pl.ds(2 * i, 2)], xs.at[pl.ds(2 * i, 2)], load_x.at[i])

    def remote(src, dst, send, recv, to):
        return pltpu.make_async_remote_copy(
            src_ref=src, dst_ref=dst, send_sem=send, recv_sem=recv, device_id=to, device_id_type=MESH
        )

    def flag_halo(way):
        return remote(flags_any, flags_by.at[way], send_f.at[way], recv_f.at[way], sides[way])

    def masked(block, k):
        return block * jnp.full(block.shape, k, jnp.float32).astype(jnp.bfloat16)

    for p in range(2):
        right[p, 1, pl.ds(layer * SB, SB), :] = jnp.zeros((SB, SB), jnp.bfloat16)
        right[p, 3, pl.ds(15 * SB + BS, BS), :] = jnp.zeros((BS, SB), jnp.bfloat16)
        right[p, 2, pl.ds((layer + 12) * SB, SB), :] = jnp.zeros((SB, SB), jnp.bfloat16)

    barrier = pltpu.get_barrier_semaphore()
    for there in sides:
        pl.semaphore_signal(barrier, inc=1, device_id=there, device_id_type=MESH)
    for k in range(1, layers):
        there = (row, col, lax.rem(layer + k, layers))
        pl.semaphore_signal(barrier, inc=1, device_id=there, device_id_type=MESH)
    pl.semaphore_wait(barrier, 2 + layers - 1)

    rows_at = lax.broadcasted_iota(jnp.int32, (BS, BS), 0)
    cols_at = lax.broadcasted_iota(jnp.int32, (BS, BS), 1)

    class Share:
        def __init__(self, l):
            self.l = l

        def x_copies(self, kind, d):
            if way_of(self.l, kind, d) is None:
                return
            i, _ = place(self.l, kind, d)
            way, _, i_there = way_of(self.l, kind, d)
            for r, q, s, n in spans(d):
                if way == 1 and 2 * i + r == 7:
                    continue
                if way == 1 and self.l == 3 and kind == 0:
                    n = 1
                yield remote(
                    x.at[2 * i + r, pl.ds(s, n)],
                    hx.at[kind, d + REACH, r, pl.ds(q, n)],
                    send_x.at[kind, d + REACH, r],
                    recv_x.at[kind, d + REACH, r],
                    sides[way],
                ), [(r, q + k, s + k) for k in range(n)]

        def x_send(self, c):
            for kind, d in chain(self.l, c):
                for copy, _ in self.x_copies(kind, d):
                    copy.start()

        def x_take(self, c):
            for kind, d in chain(self.l, (c + 2) % 4):
                for copy, brought in self.x_copies(kind, d):
                    i, _ = place(self.l, kind, d)
                    way, c_there, i_there = way_of(self.l, kind, d)
                    copy.wait_recv()
                    for r, q, s in brought:
                        k = jnp.float32(1.0) if s == W // 2 else flags_by[way, 2 * i + r, s].astype(jnp.float32)
                        at = (i_there + 4) * SB + r * BS
                        right[0, c_there, at : at + BS, q * BS : (q + 1) * BS] = masked(hx[kind, d + REACH, r, q], k)

        def t_copy(self, kind, d):
            i, c = place(self.l, kind, d)
            way, c_there, i_there = way_of(self.l, kind, d)
            first, high, wide = 0, SB, SB
            if d == REACH:
                first, high, wide = BS, BS, BS
            if way == 1 and i == 3:
                high = BS
            if way == 1 and self.l == 3 and kind == 0:
                wide = BS
            return remote(
                res.at[0, kind, d + REACH, pl.ds(first, high), pl.ds(0, wide)],
                right.at[1, c_there, pl.ds((i_there + 4) * SB + first, high), pl.ds(0, wide)],
                send_t.at[kind, d + REACH],
                recv_t.at[kind, d + REACH],
                sides[way],
            )

        def own_right(self):
            for kind in range(2):
                for d in DIAGS:
                    i, c = place(self.l, kind, d)
                    right[0, c, (i + 4) * SB : (i + 5) * SB, :] = xl[i, :, (d + REACH) * SB : (d + REACH + 1) * SB]

        def task(self, p, kind, d):
            i, c = place(self.l, kind, d)
            n, first = 9 - abs(d), max(d, 0)
            total = jnp.dot(
                xl[i, :, first * SB : (first + n) * SB],
                right[p, c, (i + first) * SB : (i + first + n) * SB, :],
                preferred_element_type=jnp.float32,
            )
            scale = jnp.where(p == 0, jnp.float32(-1.0), jnp.float32(0.5))
            three = jnp.where(rows_at == cols_at, jnp.where(p == 0, jnp.float32(3.0), jnp.float32(0.0)), jnp.float32(0.0))
            if abs(d) == REACH:
                res[p, kind, d + REACH] = jnp.zeros((SB, SB), jnp.bfloat16)
            for r, q, s in cells(d):
                part = total[r * BS : (r + 1) * BS, q * BS : (q + 1) * BS]
                part = part * scale + three if s == W // 2 else part * (scale * keep(2 * i + r, s))
                res[p, kind, d + REACH, r * BS : (r + 1) * BS, q * BS : (q + 1) * BS] = part.astype(jnp.bfloat16)

        def third_out(self, c):
            for kind, d in chain(self.l, c):
                if way_of(self.l, kind, d):
                    self.t_copy(kind, d).start()
            for kind, d in chain(self.l, c):
                i, _ = place(self.l, kind, d)
                right[1, c, (i + 4) * SB : (i + 5) * SB, :] = res[0, kind, d + REACH]

        def result_out(self, c):
            for kind, d in chain(self.l, c):
                i, _ = place(self.l, kind, d)
                for r, q, s in cells(d):
                    src = res.at[1, kind, d + REACH, pl.ds(r * BS, BS), pl.ds(q * BS, BS)]
                    dst = out.at[2 * (i & 1) + r, s]
                    if i >> 1 == self.l:
                        pltpu.make_async_copy(src, dst, own_o).start()
                    else:
                        remote(src, dst, send_o, recv_o, (row, col, i >> 1)).start()

        def t_take(self, c):
            for at in chain(self.l, (c + 2) % 4):
                if way_of(self.l, *at):
                    self.t_copy(*at).wait_recv()

        def start(self):
            def step(at, _):
                turn = jnp.where(core == 0, pick(at, (1, 3, 2, 0)), pick(at, (3, 0, 1, 2)))
                for c in range(4):
                    pl.when(turn == c)(functools.partial(self.x_send, c))
                return 0

            lax.fori_loop(0, 4, step, 0)

        def block(self, c, p):
            pl.when(p == 0)(functools.partial(self.x_take, c))
            pl.when(p == 1)(functools.partial(self.t_take, c))
            for kind, d in chain(self.l, c):
                self.task(p, kind, d)
            pl.when(p == 0)(functools.partial(self.third_out, c))
            pl.when(p == 1)(functools.partial(self.result_out, c))

        def run(self):
            self.own_right()

            def step(at, _):
                turn = [pick(at, [(c + 4 * p) for c, p in order]) for order in ORDERS]
                turn = jnp.where(core == 0, *turn)
                for c in range(4):
                    pl.when((turn & 3) == c)(functools.partial(self.block, c, turn >> 2))
                return 0

            lax.fori_loop(0, 8, step, 0)
            for c in range(4):
                for kind, d in chain(self.l, c):
                    for copy, _ in self.x_copies(kind, d):
                        copy.wait_send()
                    if way_of(self.l, kind, d):
                        self.t_copy(kind, d).wait_send()

    core = lax.rem(col, 2)

    def pick(at, values):
        out = jnp.int32(values[-1])
        for k, value in enumerate(values[:-1]):
            out = jnp.where(at == k, jnp.int32(value), out)
        return out

    def each_share(act):
        for l in range(4):
            pl.when(layer == l)(functools.partial(act, Share(l)))

    flag_halo(0).start()
    flag_halo(1).start()

    each_share(Share.start)
    for i in range(8):
        big_load(i).start()

    def fill(i, _):
        big_load(i).wait()
        none = jnp.zeros((BS, BS), jnp.bfloat16)
        for r in range(2):
            for s in range(W):
                xl[i, pl.ds(r * BS, BS), pl.ds((r + s) * BS, BS)] = masked(xs[2 * i + r, s], keep(2 * i + r, s))
        xl[i, pl.ds(0, BS), pl.ds(16 * BS, BS)] = none
        xl[i, pl.ds(0, BS), pl.ds(17 * BS, BS)] = none
        xl[i, pl.ds(BS, BS), pl.ds(0, BS)] = none
        xl[i, pl.ds(BS, BS), pl.ds(17 * BS, BS)] = none
        return 0

    lax.fori_loop(0, 8, fill, 0)
    flag_halo(0).wait()
    flag_halo(1).wait()

    each_share(Share.run)

    pltpu.make_async_copy(xs.at[pl.ds(0, 1)], out.at[pl.ds(0, 1)], own_o).wait()
    pltpu.make_async_copy(xs.at[pl.ds(0, 3)], out.at[pl.ds(0, 3)], send_o).wait()
    pltpu.make_async_copy(xs.at[pl.ds(0, 3)], out.at[pl.ds(0, 3)], recv_o).wait()


def per_device(blocks, flags):
    return pl.pallas_call(
        kernel,
        out_shape=jax.ShapeDtypeStruct((4, W, BS, BS), jnp.bfloat16),
        in_specs=[
            pl.BlockSpec(memory_space=pl.ANY),
            pl.BlockSpec(memory_space=pltpu.SMEM),
            pl.BlockSpec(memory_space=pl.ANY),
        ],
        out_specs=pl.BlockSpec(memory_space=pl.ANY),
        scratch_shapes=[
            pltpu.VMEM((2, 9, 2, 2, BS, BS), jnp.bfloat16),
            pltpu.VMEM((ROWS, W, BS, BS), jnp.bfloat16),
            pltpu.VMEM((8, SB, 9 * SB), jnp.bfloat16),
            pltpu.VMEM((2, 4, 16 * SB, SB), jnp.bfloat16),
            pltpu.VMEM((2, 2, 9, SB, SB), jnp.bfloat16),
            pltpu.SMEM((2, ROWS, W), jnp.int32),
            pltpu.SemaphoreType.DMA((8,)),
            pltpu.SemaphoreType.DMA((2,)),
            pltpu.SemaphoreType.DMA((2,)),
            pltpu.SemaphoreType.DMA((2, 9, 2)),
            pltpu.SemaphoreType.DMA((2, 9, 2)),
            pltpu.SemaphoreType.DMA((2, 9)),
            pltpu.SemaphoreType.DMA((2, 9)),
            pltpu.SemaphoreType.DMA,
            pltpu.SemaphoreType.DMA,
            pltpu.SemaphoreType.DMA,
        ],
        compiler_params=pltpu.CompilerParams(
            collective_id=0, has_side_effects=True, vmem_limit_bytes=56 * 2**20
        ),
        cost_estimate=pl.CostEstimate(
            flops=2 * 2 * 122 * SB**3, bytes_accessed=10 * 2**20, transcendentals=0
        ),
    )(blocks, flags, flags)


def solution(mesh):
    return jax.shard_map(
        per_device,
        mesh=mesh,
        in_specs=(P(("row", "col"), None, None, None), P(("row", "col"), None)),
        out_specs=P(("row", "col", "layer"), None, None, None),
        check_vma=False,
    )
```

```python
import functools

import jax
import jax.numpy as jnp
from jax import lax
from jax.experimental import pallas as pl
from jax.experimental.pallas import tpu as pltpu
from jax.sharding import PartitionSpec as P

MESH = pl.DeviceIdType.MESH
REACH = 4
DIAGS = range(-REACH, REACH + 1)
BS = 128
SB = 256
W = 16
ROWS = 16


ORDERS = (
    ((3, 0), (2, 0), (2, 1), (1, 0), (3, 1), (0, 0), (1, 1), (0, 1)),
    ((0, 0), (1, 0), (1, 1), (3, 0), (0, 1), (2, 0), (3, 1), (2, 1)),
)


def place(layer, kind, d):
    m = (d - layer + 3) >> 2
    t = (m + kind) & 1
    return layer - d + 4 * m + 4 * t, 1 + m + t


def spans(d):
    out = []
    for r in range(2):
        low, high = 2 * d - r + 8, 2 * d - r + 10
        first, last = max(low, 0), min(high, W)
        if last > first:
            out.append((r, first - low, first, last - first))
    return out


def cells(d):
    return [(r, q0 + k, s0 + k) for r, q0, s0, n in spans(d) for k in range(n)]


def chain(layer, c):
    middle = layer - 4 + 4 * c
    return [(1 - c % 2, middle - i) for i in range(max(middle - 4, 0), min(middle + 4, 7) + 1)]


def way_of(layer, kind, d):
    i, c = place(layer, kind, d)
    if c >= 2 and i >= 4:
        return 0, c - 2, i - 8
    if c <= 1 and i <= 3:
        return 1, c + 2, i + 8
    return None


def kernel(
    x, flags_any, out, hx, xs, xl, right, res, flags, flags_by, load_x,
    send_f, recv_f, send_x, recv_x, send_t, recv_t, send_o, recv_o, own_o, own_f, answer, told,
):
    row, col, layer = lax.axis_index("row"), lax.axis_index("col"), lax.axis_index("layer")
    cols, layers = lax.axis_size("col"), lax.axis_size("layer")
    groups = lax.axis_size("row") * cols
    group = row * cols + col

    def at_group(step):
        there = lax.rem(group + step + groups, groups)
        return there // cols, lax.rem(there, cols), layer

    sides = at_group(1), at_group(-1)

    def keep(i, s):
        return jnp.float32(1.0) if s == W // 2 else flags[i, s].astype(jnp.float32)

    def big_load(i):
        return pltpu.make_async_copy(x.at[pl.ds(2 * i, 2)], xs.at[pl.ds(2 * i, 2)], load_x.at[i])

    def remote(src, dst, send, recv, to):
        return pltpu.make_async_remote_copy(
            src_ref=src, dst_ref=dst, send_sem=send, recv_sem=recv, device_id=to, device_id_type=MESH
        )

    def flag_halo(way):
        return remote(flags_any, flags_by.at[way], send_f.at[way], recv_f.at[way], sides[way])

    def masked(block, k):
        return block * jnp.full(block.shape, k, jnp.float32).astype(jnp.bfloat16)

    own_flags = pltpu.make_async_copy(flags_any, flags, own_f)
    own_flags.start()
    for i in range(8):
        big_load(i).start()

    for p in range(2):
        right[p, 1, pl.ds(layer * SB, SB), :] = jnp.zeros((SB, SB), jnp.bfloat16)
        right[p, 3, pl.ds(15 * SB + BS, BS), :] = jnp.zeros((BS, SB), jnp.bfloat16)
        right[p, 2, pl.ds((layer + 12) * SB, SB), :] = jnp.zeros((SB, SB), jnp.bfloat16)

    barrier = pltpu.get_barrier_semaphore()
    core = lax.rem(col, 2)

    @pl.when(core == 0)
    def _():
        for there in sides:
            pl.semaphore_signal(barrier, inc=1, device_id=there, device_id_type=MESH)

    @pl.when(core == 1)
    def _():
        pl.semaphore_wait(barrier, 2)
        for there in sides:
            pl.semaphore_signal(answer, inc=1, device_id=there, device_id_type=MESH)

    @pl.when(core == 0)
    def _():
        pl.semaphore_wait(answer, 2)
        for k in range(1, layers):
            there = (row, col, lax.rem(layer + k, layers))
            pl.semaphore_signal(barrier, inc=1, device_id=there, device_id_type=MESH)

    def at_layers():
        @pl.when(core == 0)
        def _():
            pl.semaphore_wait(barrier, layers - 1)
            pl.semaphore_signal(told, inc=1, device_id=sides[0], device_id_type=MESH)

        @pl.when(core == 1)
        def _():
            pl.semaphore_wait(told, 1)

    rows_at = lax.broadcasted_iota(jnp.int32, (BS, BS), 0)
    cols_at = lax.broadcasted_iota(jnp.int32, (BS, BS), 1)

    class Share:
        def __init__(self, l):
            self.l = l

        def x_copies(self, kind, d):
            if way_of(self.l, kind, d) is None:
                return
            i, _ = place(self.l, kind, d)
            way, _, i_there = way_of(self.l, kind, d)
            for r, q, s, n in spans(d):
                if way == 1 and 2 * i + r == 7:
                    continue
                if way == 1 and self.l == 3 and kind == 0:
                    n = 1
                yield remote(
                    x.at[2 * i + r, pl.ds(s, n)],
                    hx.at[kind, d + REACH, r, pl.ds(q, n)],
                    send_x.at[kind, d + REACH, r],
                    recv_x.at[kind, d + REACH, r],
                    sides[way],
                ), [(r, q + k, s + k) for k in range(n)]

        def x_send(self, c):
            for kind, d in chain(self.l, c):
                for copy, _ in self.x_copies(kind, d):
                    copy.start()

        def x_take(self, c):
            for kind, d in chain(self.l, (c + 2) % 4):
                for copy, brought in self.x_copies(kind, d):
                    i, _ = place(self.l, kind, d)
                    way, c_there, i_there = way_of(self.l, kind, d)
                    copy.wait_recv()
                    for r, q, s in brought:
                        k = jnp.float32(1.0) if s == W // 2 else flags_by[way, 2 * i + r, s].astype(jnp.float32)
                        at = (i_there + 4) * SB + r * BS
                        right[0, c_there, at : at + BS, q * BS : (q + 1) * BS] = masked(hx[kind, d + REACH, r, q], k)

        def t_copy(self, kind, d):
            i, c = place(self.l, kind, d)
            way, c_there, i_there = way_of(self.l, kind, d)
            first, high, wide = 0, SB, SB
            if d == REACH:
                first, high, wide = BS, BS, BS
            if way == 1 and i == 3:
                high = BS
            if way == 1 and self.l == 3 and kind == 0:
                wide = BS
            return remote(
                right.at[1, c, pl.ds((i + 4) * SB + first, high), pl.ds(0, wide)],
                right.at[1, c_there, pl.ds((i_there + 4) * SB + first, high), pl.ds(0, wide)],
                send_t.at[kind, d + REACH],
                recv_t.at[kind, d + REACH],
                sides[way],
            )

        def own_right(self):
            for kind in range(2):
                for d in DIAGS:
                    i, c = place(self.l, kind, d)
                    right[0, c, (i + 4) * SB : (i + 5) * SB, :] = xl[i, :, (d + REACH) * SB : (d + REACH + 1) * SB]

        def task(self, p, kind, d):
            i, c = place(self.l, kind, d)
            n, first = 9 - abs(d), max(d, 0)
            total = jnp.dot(
                xl[i, :, first * SB : (first + n) * SB],
                right[p, c, (i + first) * SB : (i + first + n) * SB, :],
                preferred_element_type=jnp.float32,
            )
            scale = jnp.where(p == 0, jnp.float32(-1.0), jnp.float32(0.5))
            three = jnp.where(rows_at == cols_at, jnp.where(p == 0, jnp.float32(3.0), jnp.float32(0.0)), jnp.float32(0.0))
            for r, q, s in cells(d):
                part = total[r * BS : (r + 1) * BS, q * BS : (q + 1) * BS]
                part = part * scale + three if s == W // 2 else part * (scale * keep(2 * i + r, s))
                res[p, kind, d + REACH, r, q] = part.astype(jnp.bfloat16)

        def third_out(self, c):
            todo = chain(self.l, c)
            todo.sort(key=lambda at: way_of(self.l, *at) is None)
            for kind, d in todo:
                i, _ = place(self.l, kind, d)
                if abs(d) == REACH:
                    right[1, c, (i + 4) * SB : (i + 5) * SB, :] = jnp.zeros((SB, SB), jnp.bfloat16)
                for r, q, _ in cells(d):
                    at = (i + 4) * SB + r * BS
                    right[1, c, at : at + BS, q * BS : (q + 1) * BS] = res[0, kind, d + REACH, r, q]
                if way_of(self.l, kind, d):
                    self.t_copy(kind, d).start()

        def result_out(self, c):
            for kind, d in chain(self.l, c):
                i, _ = place(self.l, kind, d)
                for r, q, s, n in spans(d):
                    src = res.at[1, kind, d + REACH, r, pl.ds(q, n)]
                    dst = out.at[2 * (i & 1) + r, pl.ds(s, n)]
                    if i >> 1 == self.l:
                        pltpu.make_async_copy(src, dst, own_o).start()
                    else:
                        remote(src, dst, send_o, recv_o, (row, col, i >> 1)).start()

        def t_take(self, c):
            for at in chain(self.l, (c + 2) % 4):
                if way_of(self.l, *at):
                    self.t_copy(*at).wait_recv()

        def start(self):
            def step(at, _):
                turn = jnp.where(core == 0, pick(at, (1, 3, 2, 0)), pick(at, (3, 0, 1, 2)))
                for c in range(4):
                    pl.when(turn == c)(functools.partial(self.x_send, c))
                return 0

            lax.fori_loop(0, 4, step, 0)

        def block(self, c, p):
            pl.when(p == 0)(functools.partial(self.x_take, c))
            pl.when(p == 1)(functools.partial(self.t_take, c))
            for kind, d in chain(self.l, c):
                self.task(p, kind, d)
            pl.when(p == 0)(functools.partial(self.third_out, c))
            pl.when(p == 1)(functools.partial(self.result_out, c))

        def run(self):
            self.own_right()

            def step(at, _):
                turn = [pick(at, [(c + 4 * p) for c, p in order]) for order in ORDERS]
                turn = jnp.where(core == 0, *turn)
                pl.when(at == 2)(at_layers)
                for c in range(4):
                    pl.when((turn & 3) == c)(functools.partial(self.block, c, turn >> 2))
                return 0

            lax.fori_loop(0, 8, step, 0)
            for c in range(4):
                for kind, d in chain(self.l, c):
                    for copy, _ in self.x_copies(kind, d):
                        copy.wait_send()
                    if way_of(self.l, kind, d):
                        self.t_copy(kind, d).wait_send()

    def pick(at, values):
        out = jnp.int32(values[-1])
        for k, value in enumerate(values[:-1]):
            out = jnp.where(at == k, jnp.int32(value), out)
        return out

    def each_share(act):
        for l in range(4):
            pl.when(layer == l)(functools.partial(act, Share(l)))

    flag_halo(0).start()
    flag_halo(1).start()

    each_share(Share.start)

    def fill(i, _):
        big_load(i).wait()
        none = jnp.zeros((BS, BS), jnp.bfloat16)
        for r in range(2):
            for s in range(W):
                xl[i, pl.ds(r * BS, BS), pl.ds((r + s) * BS, BS)] = masked(xs[2 * i + r, s], keep(2 * i + r, s))
        xl[i, pl.ds(0, BS), pl.ds(16 * BS, BS)] = none
        xl[i, pl.ds(0, BS), pl.ds(17 * BS, BS)] = none
        xl[i, pl.ds(BS, BS), pl.ds(0, BS)] = none
        xl[i, pl.ds(BS, BS), pl.ds(17 * BS, BS)] = none
        return 0

    own_flags.wait()
    lax.fori_loop(0, 8, fill, 0)
    flag_halo(0).wait()
    flag_halo(1).wait()

    each_share(Share.run)

    pltpu.make_async_copy(xs.at[pl.ds(0, 1)], out.at[pl.ds(0, 1)], own_o).wait()
    pltpu.make_async_copy(xs.at[pl.ds(0, 3)], out.at[pl.ds(0, 3)], send_o).wait()
    pltpu.make_async_copy(xs.at[pl.ds(0, 3)], out.at[pl.ds(0, 3)], recv_o).wait()


def per_device(blocks, flags):
    return pl.pallas_call(
        kernel,
        out_shape=jax.ShapeDtypeStruct((4, W, BS, BS), jnp.bfloat16),
        in_specs=[
            pl.BlockSpec(memory_space=pl.ANY),
            pl.BlockSpec(memory_space=pl.ANY),
        ],
        out_specs=pl.BlockSpec(memory_space=pl.ANY),
        scratch_shapes=[
            pltpu.VMEM((2, 9, 2, 2, BS, BS), jnp.bfloat16),
            pltpu.VMEM((ROWS, W, BS, BS), jnp.bfloat16),
            pltpu.VMEM((8, SB, 9 * SB), jnp.bfloat16),
            pltpu.VMEM((2, 4, 16 * SB, SB), jnp.bfloat16),
            pltpu.VMEM((2, 2, 9, 2, 2, BS, BS), jnp.bfloat16),
            pltpu.SMEM((ROWS, W), jnp.int32),
            pltpu.SMEM((2, ROWS, W), jnp.int32),
            pltpu.SemaphoreType.DMA((8,)),
            pltpu.SemaphoreType.DMA((2,)),
            pltpu.SemaphoreType.DMA((2,)),
            pltpu.SemaphoreType.DMA((2, 9, 2)),
            pltpu.SemaphoreType.DMA((2, 9, 2)),
            pltpu.SemaphoreType.DMA((2, 9)),
            pltpu.SemaphoreType.DMA((2, 9)),
            pltpu.SemaphoreType.DMA,
            pltpu.SemaphoreType.DMA,
            pltpu.SemaphoreType.DMA,
            pltpu.SemaphoreType.DMA,
            pltpu.SemaphoreType.REGULAR,
            pltpu.SemaphoreType.REGULAR,
        ],
        compiler_params=pltpu.CompilerParams(
            collective_id=0, has_side_effects=True, vmem_limit_bytes=56 * 2**20
        ),
        cost_estimate=pl.CostEstimate(
            flops=2 * 2 * 122 * SB**3, bytes_accessed=10 * 2**20, transcendentals=0
        ),
    )(blocks, flags)


def solution(mesh):
    return jax.shard_map(
        per_device,
        mesh=mesh,
        in_specs=(P(("row", "col"), None, None, None), P(("row", "col"), None)),
        out_specs=P(("row", "col", "layer"), None, None, None),
        check_vma=False,
    )
```

```python
import functools

import jax
import jax.numpy as jnp
from jax import lax
from jax.experimental import pallas as pl
from jax.experimental.pallas import tpu as pltpu
from jax.sharding import PartitionSpec as P

MESH = pl.DeviceIdType.MESH
REACH = 4
DIAGS = range(-REACH, REACH + 1)
BS = 128
SB = 256
W = 16
ROWS = 16


ORDERS = (
    ((3, 0), (2, 0), (2, 1), (3, 1), (1, 0), (0, 0), (1, 1), (0, 1)),
    ((0, 0), (1, 0), (1, 1), (0, 1), (3, 0), (2, 0), (3, 1), (2, 1)),
)


def place(layer, kind, d):
    m = (d - layer + 3) >> 2
    t = (m + kind) & 1
    return layer - d + 4 * m + 4 * t, 1 + m + t


def spans(d):
    out = []
    for r in range(2):
        low, high = 2 * d - r + 8, 2 * d - r + 10
        first, last = max(low, 0), min(high, W)
        if last > first:
            out.append((r, first - low, first, last - first))
    return out


def cells(d):
    return [(r, q0 + k, s0 + k) for r, q0, s0, n in spans(d) for k in range(n)]


def chain(layer, c):
    middle = layer - 4 + 4 * c
    return [(1 - c % 2, middle - i) for i in range(max(middle - 4, 0), min(middle + 4, 7) + 1)]


def way_of(layer, kind, d):
    i, c = place(layer, kind, d)
    if c >= 2 and i >= 4:
        return 0, c - 2, i - 8
    if c <= 1 and i <= 3:
        return 1, c + 2, i + 8
    return None


def kernel(
    x, flags_any, out, hx, xs, xl, right, res, flags, flags_by, load_x,
    send_f, recv_f, send_x, recv_x, send_t, recv_t, send_o, recv_o, own_o, own_f, answer, told,
):
    row, col, layer = lax.axis_index("row"), lax.axis_index("col"), lax.axis_index("layer")
    cols, layers = lax.axis_size("col"), lax.axis_size("layer")
    groups = lax.axis_size("row") * cols
    group = row * cols + col

    def at_group(step):
        there = lax.rem(group + step + groups, groups)
        return there // cols, lax.rem(there, cols), layer

    sides = at_group(1), at_group(-1)

    def keep(i, s):
        return jnp.float32(1.0) if s == W // 2 else flags[i, s].astype(jnp.float32)

    def big_load(i):
        return pltpu.make_async_copy(x.at[pl.ds(2 * i, 2)], xs.at[pl.ds(2 * i, 2)], load_x.at[i])

    def remote(src, dst, send, recv, to):
        return pltpu.make_async_remote_copy(
            src_ref=src, dst_ref=dst, send_sem=send, recv_sem=recv, device_id=to, device_id_type=MESH
        )

    def flag_halo(way):
        return remote(flags_any, flags_by.at[way], send_f.at[way], recv_f.at[way], sides[way])

    def masked(block, k):
        return block * jnp.full(block.shape, k, jnp.float32).astype(jnp.bfloat16)

    own_flags = pltpu.make_async_copy(flags_any, flags, own_f)
    own_flags.start()
    for i in range(8):
        big_load(i).start()

    for p in range(2):
        right[p, 1, pl.ds(layer * SB, SB), :] = jnp.zeros((SB, SB), jnp.bfloat16)
        right[p, 3, pl.ds(15 * SB + BS, BS), :] = jnp.zeros((BS, SB), jnp.bfloat16)
        right[p, 2, pl.ds((layer + 12) * SB, SB), :] = jnp.zeros((SB, SB), jnp.bfloat16)

    barrier = pltpu.get_barrier_semaphore()
    core = lax.rem(col, 2)

    @pl.when(core == 0)
    def _():
        for there in sides:
            pl.semaphore_signal(barrier, inc=1, device_id=there, device_id_type=MESH)

    @pl.when(core == 1)
    def _():
        pl.semaphore_wait(barrier, 2)
        for there in sides:
            pl.semaphore_signal(answer, inc=1, device_id=there, device_id_type=MESH)

    @pl.when(core == 0)
    def _():
        pl.semaphore_wait(answer, 2)
        for k in range(1, layers):
            there = (row, col, lax.rem(layer + k, layers))
            pl.semaphore_signal(barrier, inc=1, device_id=there, device_id_type=MESH)

    def at_layers():
        @pl.when(core == 0)
        def _():
            pl.semaphore_wait(barrier, layers - 1)
            pl.semaphore_signal(told, inc=1, device_id=sides[0], device_id_type=MESH)

        @pl.when(core == 1)
        def _():
            pl.semaphore_wait(told, 1)

    rows_at = lax.broadcasted_iota(jnp.int32, (BS, BS), 0)
    cols_at = lax.broadcasted_iota(jnp.int32, (BS, BS), 1)

    class Share:
        def __init__(self, l):
            self.l = l

        def x_copies(self, kind, d):
            if way_of(self.l, kind, d) is None:
                return
            i, _ = place(self.l, kind, d)
            way, _, i_there = way_of(self.l, kind, d)
            for r, q, s, n in spans(d):
                if way == 1 and 2 * i + r == 7:
                    continue
                if way == 1 and self.l == 3 and kind == 0:
                    n = 1
                yield remote(
                    x.at[2 * i + r, pl.ds(s, n)],
                    hx.at[kind, d + REACH, r, pl.ds(q, n)],
                    send_x.at[kind, d + REACH, r],
                    recv_x.at[kind, d + REACH, r],
                    sides[way],
                ), [(r, q + k, s + k) for k in range(n)]

        def x_send(self, c):
            for kind, d in chain(self.l, c):
                for copy, _ in self.x_copies(kind, d):
                    copy.start()

        def x_take(self, c):
            for kind, d in chain(self.l, (c + 2) % 4):
                for copy, brought in self.x_copies(kind, d):
                    i, _ = place(self.l, kind, d)
                    way, c_there, i_there = way_of(self.l, kind, d)
                    copy.wait_recv()
                    for r, q, s in brought:
                        k = jnp.float32(1.0) if s == W // 2 else flags_by[way, 2 * i + r, s].astype(jnp.float32)
                        at = (i_there + 4) * SB + r * BS
                        right[0, c_there, at : at + BS, q * BS : (q + 1) * BS] = masked(hx[kind, d + REACH, r, q], k)

        def t_copy(self, kind, d):
            i, c = place(self.l, kind, d)
            way, c_there, i_there = way_of(self.l, kind, d)
            first, high, wide = 0, SB, SB
            if d == REACH:
                first, high, wide = BS, BS, BS
            if way == 1 and i == 3:
                high = BS
            if way == 1 and self.l == 3 and kind == 0:
                wide = BS
            return remote(
                right.at[1, c, pl.ds((i + 4) * SB + first, high), pl.ds(0, wide)],
                right.at[1, c_there, pl.ds((i_there + 4) * SB + first, high), pl.ds(0, wide)],
                send_t.at[kind, d + REACH],
                recv_t.at[kind, d + REACH],
                sides[way],
            )

        def own_right(self):
            for kind in range(2):
                for d in DIAGS:
                    i, c = place(self.l, kind, d)
                    right[0, c, (i + 4) * SB : (i + 5) * SB, :] = xl[i, :, (d + REACH) * SB : (d + REACH + 1) * SB]

        def task(self, p, kind, d):
            i, c = place(self.l, kind, d)
            n, first = 9 - abs(d), max(d, 0)
            total = jnp.dot(
                xl[i, :, first * SB : (first + n) * SB],
                right[p, c, (i + first) * SB : (i + first + n) * SB, :],
                preferred_element_type=jnp.float32,
            )
            scale = jnp.where(p == 0, jnp.float32(-1.0), jnp.float32(0.5))
            three = jnp.where(rows_at == cols_at, jnp.where(p == 0, jnp.float32(3.0), jnp.float32(0.0)), jnp.float32(0.0))
            for r, q, s in cells(d):
                part = total[r * BS : (r + 1) * BS, q * BS : (q + 1) * BS]
                part = part * scale + three if s == W // 2 else part * (scale * keep(2 * i + r, s))
                res[p, kind, d + REACH, r, q] = part.astype(jnp.bfloat16)

        def third_out(self, c):
            todo = chain(self.l, c)
            todo.sort(key=lambda at: way_of(self.l, *at) is None)
            for kind, d in todo:
                i, _ = place(self.l, kind, d)
                if abs(d) == REACH:
                    right[1, c, (i + 4) * SB : (i + 5) * SB, :] = jnp.zeros((SB, SB), jnp.bfloat16)
                for r, q, _ in cells(d):
                    at = (i + 4) * SB + r * BS
                    right[1, c, at : at + BS, q * BS : (q + 1) * BS] = res[0, kind, d + REACH, r, q]
                if way_of(self.l, kind, d):
                    self.t_copy(kind, d).start()

        def result_out(self, c):
            for kind, d in chain(self.l, c):
                i, _ = place(self.l, kind, d)
                for r, q, s, n in spans(d):
                    src = res.at[1, kind, d + REACH, r, pl.ds(q, n)]
                    dst = out.at[2 * (i & 1) + r, pl.ds(s, n)]
                    if i >> 1 == self.l:
                        pltpu.make_async_copy(src, dst, own_o).start()
                    else:
                        remote(src, dst, send_o, recv_o, (row, col, i >> 1)).start()

        def t_take(self, c):
            for at in chain(self.l, (c + 2) % 4):
                if way_of(self.l, *at):
                    self.t_copy(*at).wait_recv()

        def start(self):
            def step(at, _):
                turn = jnp.where(core == 0, pick(at, (1, 3, 2, 0)), pick(at, (3, 0, 1, 2)))
                for c in range(4):
                    pl.when(turn == c)(functools.partial(self.x_send, c))
                return 0

            lax.fori_loop(0, 4, step, 0)

        def block(self, c, p):
            pl.when(p == 0)(functools.partial(self.x_take, c))
            pl.when(p == 1)(functools.partial(self.t_take, c))
            for kind, d in chain(self.l, c):
                self.task(p, kind, d)
            pl.when(p == 0)(functools.partial(self.third_out, c))
            pl.when(p == 1)(functools.partial(self.result_out, c))

        def run(self):
            self.own_right()

            def step(at, _):
                turn = [pick(at, [(c + 4 * p) for c, p in order]) for order in ORDERS]
                turn = jnp.where(core == 0, *turn)
                pl.when(at == 2)(at_layers)
                for c in range(4):
                    pl.when((turn & 3) == c)(functools.partial(self.block, c, turn >> 2))
                return 0

            lax.fori_loop(0, 8, step, 0)
            for c in range(4):
                for kind, d in chain(self.l, c):
                    for copy, _ in self.x_copies(kind, d):
                        copy.wait_send()
                    if way_of(self.l, kind, d):
                        self.t_copy(kind, d).wait_send()

    def pick(at, values):
        out = jnp.int32(values[-1])
        for k, value in enumerate(values[:-1]):
            out = jnp.where(at == k, jnp.int32(value), out)
        return out

    def each_share(act):
        for l in range(4):
            pl.when(layer == l)(functools.partial(act, Share(l)))

    flag_halo(0).start()
    flag_halo(1).start()

    each_share(Share.start)

    def fill(i, _):
        big_load(i).wait()
        none = jnp.zeros((BS, BS), jnp.bfloat16)
        for r in range(2):
            for s in range(W):
                xl[i, pl.ds(r * BS, BS), pl.ds((r + s) * BS, BS)] = masked(xs[2 * i + r, s], keep(2 * i + r, s))
        xl[i, pl.ds(0, BS), pl.ds(16 * BS, BS)] = none
        xl[i, pl.ds(0, BS), pl.ds(17 * BS, BS)] = none
        xl[i, pl.ds(BS, BS), pl.ds(0, BS)] = none
        xl[i, pl.ds(BS, BS), pl.ds(17 * BS, BS)] = none
        return 0

    own_flags.wait()
    lax.fori_loop(0, 8, fill, 0)
    flag_halo(0).wait()
    flag_halo(1).wait()

    each_share(Share.run)

    pltpu.make_async_copy(xs.at[pl.ds(0, 1)], out.at[pl.ds(0, 1)], own_o).wait()
    pltpu.make_async_copy(xs.at[pl.ds(0, 3)], out.at[pl.ds(0, 3)], send_o).wait()
    pltpu.make_async_copy(xs.at[pl.ds(0, 3)], out.at[pl.ds(0, 3)], recv_o).wait()


def iterate(blocks, flags):
    return pl.pallas_call(
        kernel,
        out_shape=jax.ShapeDtypeStruct((4, W, BS, BS), jnp.bfloat16),
        in_specs=[
            pl.BlockSpec(memory_space=pl.ANY),
            pl.BlockSpec(memory_space=pl.ANY),
        ],
        out_specs=pl.BlockSpec(memory_space=pl.ANY),
        scratch_shapes=[
            pltpu.VMEM((2, 9, 2, 2, BS, BS), jnp.bfloat16),
            pltpu.VMEM((ROWS, W, BS, BS), jnp.bfloat16),
            pltpu.VMEM((8, SB, 9 * SB), jnp.bfloat16),
            pltpu.VMEM((2, 4, 16 * SB, SB), jnp.bfloat16),
            pltpu.VMEM((2, 2, 9, 2, 2, BS, BS), jnp.bfloat16),
            pltpu.SMEM((ROWS, W), jnp.int32),
            pltpu.SMEM((2, ROWS, W), jnp.int32),
            pltpu.SemaphoreType.DMA((8,)),
            pltpu.SemaphoreType.DMA((2,)),
            pltpu.SemaphoreType.DMA((2,)),
            pltpu.SemaphoreType.DMA((2, 9, 2)),
            pltpu.SemaphoreType.DMA((2, 9, 2)),
            pltpu.SemaphoreType.DMA((2, 9)),
            pltpu.SemaphoreType.DMA((2, 9)),
            pltpu.SemaphoreType.DMA,
            pltpu.SemaphoreType.DMA,
            pltpu.SemaphoreType.DMA,
            pltpu.SemaphoreType.DMA,
            pltpu.SemaphoreType.REGULAR,
            pltpu.SemaphoreType.REGULAR,
        ],
        compiler_params=pltpu.CompilerParams(
            collective_id=0, has_side_effects=True, vmem_limit_bytes=56 * 2**20
        ),
        cost_estimate=pl.CostEstimate(
            flops=2 * 2 * 122 * SB**3, bytes_accessed=10 * 2**20, transcendentals=0
        ),
    )(blocks, flags)


def settle(src, dst, held, sem_in, sem_out):
    pieces = [(k // 2, pl.ds(k % 2 * 8, 8)) for k in range(8)]
    reads = [pltpu.make_async_copy(src.at[at], held.at[at], sem_in.at[k]) for k, at in enumerate(pieces)]
    writes = [pltpu.make_async_copy(held.at[at], dst.at[at], sem_out.at[k]) for k, at in enumerate(pieces)]
    for read in reads:
        read.start()
    for read, write in zip(reads, writes):
        read.wait()
        write.start()
    for write in writes:
        write.wait()


def per_device(blocks, flags):
    result = iterate(blocks, flags)
    return pl.pallas_call(
        settle,
        out_shape=jax.ShapeDtypeStruct(result.shape, result.dtype),
        in_specs=[pl.BlockSpec(memory_space=pl.ANY)],
        out_specs=pl.BlockSpec(memory_space=pl.ANY),
        scratch_shapes=[
            pltpu.VMEM(result.shape, result.dtype),
            pltpu.SemaphoreType.DMA((8,)),
            pltpu.SemaphoreType.DMA((8,)),
        ],
    )(result)


def solution(mesh):
    return jax.shard_map(
        per_device,
        mesh=mesh,
        in_specs=(P(("row", "col"), None, None, None), P(("row", "col"), None)),
        out_specs=P(("row", "col", "layer"), None, None, None),
        check_vma=False,
    )
```

```python
import functools

import jax
import jax.numpy as jnp
from jax import lax
from jax.experimental import pallas as pl
from jax.experimental.pallas import tpu as pltpu
from jax.sharding import PartitionSpec as P

MESH = pl.DeviceIdType.MESH
REACH = 4
DIAGS = range(-REACH, REACH + 1)
BS = 128
SB = 256
W = 16
ROWS = 16


ORDERS = (
    ((3, 0), (2, 0), (2, 1), (3, 1), (1, 0), (0, 0), (1, 1), (0, 1)),
    ((0, 0), (1, 0), (1, 1), (0, 1), (3, 0), (2, 0), (3, 1), (2, 1)),
)


def place(layer, kind, d):
    m = (d - layer + 3) >> 2
    t = (m + kind) & 1
    return layer - d + 4 * m + 4 * t, 1 + m + t


def spans(d):
    out = []
    for r in range(2):
        low, high = 2 * d - r + 8, 2 * d - r + 10
        first, last = max(low, 0), min(high, W)
        if last > first:
            out.append((r, first - low, first, last - first))
    return out


def cells(d):
    return [(r, q0 + k, s0 + k) for r, q0, s0, n in spans(d) for k in range(n)]


def chain(layer, c):
    middle = layer - 4 + 4 * c
    return [(1 - c % 2, middle - i) for i in range(max(middle - 4, 0), min(middle + 4, 7) + 1)]


def way_of(layer, kind, d):
    i, c = place(layer, kind, d)
    if c >= 2 and i >= 4:
        return 0, c - 2, i - 8
    if c <= 1 and i <= 3:
        return 1, c + 2, i + 8
    return None


def kernel(
    x, flags_any, out, hx, xs, xl, right, res, flags, flags_by, load_x,
    send_f, recv_f, send_x, recv_x, send_t, recv_t, send_o, recv_o, own_o, own_f, answer, told,
):
    row, col, layer = lax.axis_index("row"), lax.axis_index("col"), lax.axis_index("layer")
    cols, layers = lax.axis_size("col"), lax.axis_size("layer")
    groups = lax.axis_size("row") * cols
    group = row * cols + col

    def at_group(step):
        there = lax.rem(group + step + groups, groups)
        return there // cols, lax.rem(there, cols), layer

    sides = at_group(1), at_group(-1)

    def keep(i, s):
        return jnp.float32(1.0) if s == W // 2 else flags[i, s].astype(jnp.float32)

    def big_load(i):
        return pltpu.make_async_copy(x.at[pl.ds(2 * i, 2)], xs.at[pl.ds(2 * i, 2)], load_x.at[i])

    def remote(src, dst, send, recv, to):
        return pltpu.make_async_remote_copy(
            src_ref=src, dst_ref=dst, send_sem=send, recv_sem=recv, device_id=to, device_id_type=MESH
        )

    def flag_halo(way):
        return remote(flags_any, flags_by.at[way], send_f.at[way], recv_f.at[way], sides[way])

    def masked(block, k):
        return block * jnp.full(block.shape, k, jnp.float32).astype(jnp.bfloat16)

    own_flags = pltpu.make_async_copy(flags_any, flags, own_f)
    own_flags.start()
    for i in range(8):
        big_load(i).start()

    for p in range(2):
        right[p, 1, pl.ds(layer * SB, SB), :] = jnp.zeros((SB, SB), jnp.bfloat16)
        right[p, 3, pl.ds(15 * SB + BS, BS), :] = jnp.zeros((BS, SB), jnp.bfloat16)
        right[p, 2, pl.ds((layer + 12) * SB, SB), :] = jnp.zeros((SB, SB), jnp.bfloat16)

    barrier = pltpu.get_barrier_semaphore()
    core = lax.rem(col, 2)

    @pl.when(core == 0)
    def _():
        for there in sides:
            pl.semaphore_signal(barrier, inc=1, device_id=there, device_id_type=MESH)

    @pl.when(core == 1)
    def _():
        pl.semaphore_wait(barrier, 2)
        for there in sides:
            pl.semaphore_signal(answer, inc=1, device_id=there, device_id_type=MESH)

    @pl.when(core == 0)
    def _():
        pl.semaphore_wait(answer, 2)
        for k in range(1, layers):
            there = (row, col, lax.rem(layer + k, layers))
            pl.semaphore_signal(barrier, inc=1, device_id=there, device_id_type=MESH)

    def at_layers():
        @pl.when(core == 0)
        def _():
            pl.semaphore_wait(barrier, layers - 1)
            pl.semaphore_signal(told, inc=1, device_id=sides[0], device_id_type=MESH)

        @pl.when(core == 1)
        def _():
            pl.semaphore_wait(told, 1)

    rows_at = lax.broadcasted_iota(jnp.int32, (BS, BS), 0)
    cols_at = lax.broadcasted_iota(jnp.int32, (BS, BS), 1)

    class Share:
        def __init__(self, l):
            self.l = l

        def x_copies(self, kind, d):
            if way_of(self.l, kind, d) is None:
                return
            i, _ = place(self.l, kind, d)
            way, _, i_there = way_of(self.l, kind, d)
            for r, q, s, n in spans(d):
                if way == 1 and 2 * i + r == 7:
                    continue
                if way == 1 and self.l == 3 and kind == 0:
                    n = 1
                yield remote(
                    x.at[2 * i + r, pl.ds(s, n)],
                    hx.at[kind, d + REACH, r, pl.ds(q, n)],
                    send_x.at[kind, d + REACH, r],
                    recv_x.at[kind, d + REACH, r],
                    sides[way],
                ), [(r, q + k, s + k) for k in range(n)]

        def x_send(self, c):
            for kind, d in chain(self.l, c):
                for copy, _ in self.x_copies(kind, d):
                    copy.start()

        def x_take(self, c):
            for kind, d in chain(self.l, (c + 2) % 4):
                for copy, brought in self.x_copies(kind, d):
                    i, _ = place(self.l, kind, d)
                    way, c_there, i_there = way_of(self.l, kind, d)
                    copy.wait_recv()
                    for r, q, s in brought:
                        k = jnp.float32(1.0) if s == W // 2 else flags_by[way, 2 * i + r, s].astype(jnp.float32)
                        at = (i_there + 4) * SB + r * BS
                        right[0, c_there, at : at + BS, q * BS : (q + 1) * BS] = masked(hx[kind, d + REACH, r, q], k)

        def t_copy(self, kind, d):
            i, c = place(self.l, kind, d)
            way, c_there, i_there = way_of(self.l, kind, d)
            first, high, wide = 0, SB, SB
            if d == REACH:
                first, high, wide = BS, BS, BS
            if way == 1 and i == 3:
                high = BS
            if way == 1 and self.l == 3 and kind == 0:
                wide = BS
            return remote(
                right.at[1, c, pl.ds((i + 4) * SB + first, high), pl.ds(0, wide)],
                right.at[1, c_there, pl.ds((i_there + 4) * SB + first, high), pl.ds(0, wide)],
                send_t.at[kind, d + REACH],
                recv_t.at[kind, d + REACH],
                sides[way],
            )

        def own_right(self):
            for kind in range(2):
                for d in DIAGS:
                    i, c = place(self.l, kind, d)
                    right[0, c, (i + 4) * SB : (i + 5) * SB, :] = xl[i, :, (d + REACH) * SB : (d + REACH + 1) * SB]

        def task(self, p, kind, d):
            i, c = place(self.l, kind, d)
            n, first = 9 - abs(d), max(d, 0)
            total = jnp.dot(
                xl[i, :, first * SB : (first + n) * SB],
                right[p, c, (i + first) * SB : (i + first + n) * SB, :],
                preferred_element_type=jnp.float32,
            )
            scale = jnp.where(p == 0, jnp.float32(-1.0), jnp.float32(0.5))
            three = jnp.where(rows_at == cols_at, jnp.where(p == 0, jnp.float32(3.0), jnp.float32(0.0)), jnp.float32(0.0))
            for r, q, s in cells(d):
                part = total[r * BS : (r + 1) * BS, q * BS : (q + 1) * BS]
                part = part * scale + three if s == W // 2 else part * (scale * keep(2 * i + r, s))
                res[p, kind, d + REACH, r, q] = part.astype(jnp.bfloat16)

        def third_out(self, c):
            todo = chain(self.l, c)
            todo.sort(key=lambda at: way_of(self.l, *at) is None)
            for kind, d in todo:
                i, _ = place(self.l, kind, d)
                if abs(d) == REACH:
                    right[1, c, (i + 4) * SB : (i + 5) * SB, :] = jnp.zeros((SB, SB), jnp.bfloat16)
                for r, q, _ in cells(d):
                    at = (i + 4) * SB + r * BS
                    right[1, c, at : at + BS, q * BS : (q + 1) * BS] = res[0, kind, d + REACH, r, q]
                if way_of(self.l, kind, d):
                    self.t_copy(kind, d).start()

        def result_out(self, c):
            for kind, d in chain(self.l, c):
                i, _ = place(self.l, kind, d)
                for r, q, s, n in spans(d):
                    src = res.at[1, kind, d + REACH, r, pl.ds(q, n)]
                    dst = out.at[2 * (i & 1) + r, pl.ds(s, n)]
                    if i >> 1 == self.l:
                        pltpu.make_async_copy(src, dst, own_o).start()
                    else:
                        remote(src, dst, send_o, recv_o, (row, col, i >> 1)).start()

        def t_take(self, c):
            for at in chain(self.l, (c + 2) % 4):
                if way_of(self.l, *at):
                    self.t_copy(*at).wait_recv()

        def start(self):
            def step(at, _):
                turn = jnp.where(core == 0, pick(at, (3, 2, 1, 0)), pick(at, (0, 1, 3, 2)))
                for c in range(4):
                    pl.when(turn == c)(functools.partial(self.x_send, c))
                return 0

            lax.fori_loop(0, 4, step, 0)

        def block(self, c, p):
            pl.when(p == 0)(functools.partial(self.x_take, c))
            pl.when(p == 1)(functools.partial(self.t_take, c))
            for kind, d in sorted(chain(self.l, c), key=lambda at: place(self.l, *at)[0] >> 1 == self.l):
                self.task(p, kind, d)
            pl.when(p == 0)(functools.partial(self.third_out, c))
            pl.when(p == 1)(functools.partial(self.result_out, c))

        def run(self):
            self.own_right()

            def step(at, _):
                turn = [pick(at, [(c + 4 * p) for c, p in order]) for order in ORDERS]
                turn = jnp.where(core == 0, *turn)
                pl.when(at == 2)(at_layers)
                for c in range(4):
                    pl.when((turn & 3) == c)(functools.partial(self.block, c, turn >> 2))
                return 0

            lax.fori_loop(0, 8, step, 0)
            for c in range(4):
                for kind, d in chain(self.l, c):
                    for copy, _ in self.x_copies(kind, d):
                        copy.wait_send()
                    if way_of(self.l, kind, d):
                        self.t_copy(kind, d).wait_send()

    def pick(at, values):
        out = jnp.int32(values[-1])
        for k, value in enumerate(values[:-1]):
            out = jnp.where(at == k, jnp.int32(value), out)
        return out

    def each_share(act):
        for l in range(4):
            pl.when(layer == l)(functools.partial(act, Share(l)))

    flag_halo(0).start()
    flag_halo(1).start()

    each_share(Share.start)

    def fill(i, _):
        big_load(i).wait()
        none = jnp.zeros((BS, BS), jnp.bfloat16)
        for r in range(2):
            for s in range(W):
                xl[i, pl.ds(r * BS, BS), pl.ds((r + s) * BS, BS)] = masked(xs[2 * i + r, s], keep(2 * i + r, s))
        xl[i, pl.ds(0, BS), pl.ds(16 * BS, BS)] = none
        xl[i, pl.ds(0, BS), pl.ds(17 * BS, BS)] = none
        xl[i, pl.ds(BS, BS), pl.ds(0, BS)] = none
        xl[i, pl.ds(BS, BS), pl.ds(17 * BS, BS)] = none
        return 0

    own_flags.wait()
    lax.fori_loop(0, 8, fill, 0)
    flag_halo(0).wait()
    flag_halo(1).wait()

    each_share(Share.run)

    pltpu.make_async_copy(xs.at[pl.ds(0, 1)], out.at[pl.ds(0, 1)], own_o).wait()
    pltpu.make_async_copy(xs.at[pl.ds(0, 3)], out.at[pl.ds(0, 3)], send_o).wait()
    pltpu.make_async_copy(xs.at[pl.ds(0, 3)], out.at[pl.ds(0, 3)], recv_o).wait()


def iterate(blocks, flags):
    return pl.pallas_call(
        kernel,
        out_shape=jax.ShapeDtypeStruct((4, W, BS, BS), jnp.bfloat16),
        in_specs=[
            pl.BlockSpec(memory_space=pl.ANY),
            pl.BlockSpec(memory_space=pl.ANY),
        ],
        out_specs=pl.BlockSpec(memory_space=pl.ANY),
        scratch_shapes=[
            pltpu.VMEM((2, 9, 2, 2, BS, BS), jnp.bfloat16),
            pltpu.VMEM((ROWS, W, BS, BS), jnp.bfloat16),
            pltpu.VMEM((8, SB, 9 * SB), jnp.bfloat16),
            pltpu.VMEM((2, 4, 16 * SB, SB), jnp.bfloat16),
            pltpu.VMEM((2, 2, 9, 2, 2, BS, BS), jnp.bfloat16),
            pltpu.SMEM((ROWS, W), jnp.int32),
            pltpu.SMEM((2, ROWS, W), jnp.int32),
            pltpu.SemaphoreType.DMA((8,)),
            pltpu.SemaphoreType.DMA((2,)),
            pltpu.SemaphoreType.DMA((2,)),
            pltpu.SemaphoreType.DMA((2, 9, 2)),
            pltpu.SemaphoreType.DMA((2, 9, 2)),
            pltpu.SemaphoreType.DMA((2, 9)),
            pltpu.SemaphoreType.DMA((2, 9)),
            pltpu.SemaphoreType.DMA,
            pltpu.SemaphoreType.DMA,
            pltpu.SemaphoreType.DMA,
            pltpu.SemaphoreType.DMA,
            pltpu.SemaphoreType.REGULAR,
            pltpu.SemaphoreType.REGULAR,
        ],
        compiler_params=pltpu.CompilerParams(
            collective_id=0, has_side_effects=True, vmem_limit_bytes=56 * 2**20
        ),
        cost_estimate=pl.CostEstimate(
            flops=2 * 2 * 122 * SB**3, bytes_accessed=10 * 2**20, transcendentals=0
        ),
    )(blocks, flags)


def settle(src, dst, held, sem_in, sem_out):
    pieces = [(k // 2, pl.ds(k % 2 * 8, 8)) for k in range(8)]
    reads = [pltpu.make_async_copy(src.at[at], held.at[at], sem_in.at[k]) for k, at in enumerate(pieces)]
    writes = [pltpu.make_async_copy(held.at[at], dst.at[at], sem_out.at[k]) for k, at in enumerate(pieces)]
    for read in reads:
        read.start()
    for read, write in zip(reads, writes):
        read.wait()
        write.start()
    for write in writes:
        write.wait()


def per_device(blocks, flags):
    result = iterate(blocks, flags)
    return pl.pallas_call(
        settle,
        out_shape=jax.ShapeDtypeStruct(result.shape, result.dtype),
        in_specs=[pl.BlockSpec(memory_space=pl.ANY)],
        out_specs=pl.BlockSpec(memory_space=pl.ANY),
        scratch_shapes=[
            pltpu.VMEM(result.shape, result.dtype),
            pltpu.SemaphoreType.DMA((8,)),
            pltpu.SemaphoreType.DMA((8,)),
        ],
    )(result)


def solution(mesh):
    return jax.shard_map(
        per_device,
        mesh=mesh,
        in_specs=(P(("row", "col"), None, None, None), P(("row", "col"), None)),
        out_specs=P(("row", "col", "layer"), None, None, None),
        check_vma=False,
    )
```
